32 devices in a mesh: groups: 2 (over x), hid: 16 (over z, y, core).
Axes of the slice: x: 2, y: 2, z: 4, core: 2. Of those that a mesh axis runs over, the one named last changes fastest.
Arguments:
- tokens: bfloat16 [8, 32, 6144], P('groups', 'hid'), parts along dimension 0, may hold values from -6 to 6
- w_gate: bfloat16 [4, 6144, 8192], P(None, None, 'hid'), may hold values from -0.078125 to 0.078125
- w_up: bfloat16 [4, 6144, 8192], P(None, None, 'hid'), may hold values from -0.078125 to 0.078125
- w_down: bfloat16 [4, 8192, 6144], P(None, 'hid'), may hold values from -0.0625 to 0.0625
- expert_ids: int32 [8, 32, 2], P('groups'), parts along dimension 0, may hold values from 0 to 3, all different within a row
- gate_weights: bfloat16 [8, 32, 2], P('groups'), parts along dimension 0, may hold values from 0.099609375 to 0.8984375
- return_order: int32 [8, 32], P('groups'), parts along dimension 0, may hold values from 0 to 31, each once within a row
Outputs:
- expert_out: bfloat16 [8, 32, 6144], P('groups', 'hid'), parts along dimension 0
The draws below stay inside these ranges and needn't reach their ends.
There are 2 independent parts, one for each index of `groups`. The reference program is written for one: setup_inputs(seed, part) draws one part's arguments, and reference() takes and returns one part's arrays. A program takes and returns all parts, laid end to end along the dimension named above; an argument that names none is the same for every part. Nothing has to cross between parts.
Inputs may be any that keep to these rules, and one draw needn't show every extreme that they name: `expert_ids`: each row names 2 different experts. `return_order`: each step's row is a permutation of the 32 rows.
All inputs are finite; a program needn't handle non-finite values.
Results may differ from the reference program's by a relative error of at most 0.0049.
Values may be sent and summed in bfloat16 or wider, within the bound.
No kernel may reach another device: no remote copies, remote signals or barrier semaphores. Data moves between devices by JAX's collectives and lax.ppermute only.
A program may use at most 192 MiB of HBM per device.

```python
import jax
import jax.numpy as jnp
from jax import lax

D = 6144
FF = 8192
E = 4
TOPK = 2
STEPS = 4
ROWS = 32


def block_scale(key, extent, pieces, low, largest):
    def one(axis_at, parts):
        draws = jax.random.uniform(jax.random.fold_in(jax.random.fold_in(key, 6), axis_at), (parts,), jnp.float32, low / len(pieces), largest / len(pieces))
        return jnp.repeat(jnp.exp(draws), extent[axis_at] // parts).reshape((-1,) + (1,) * (len(extent) - axis_at - 1))

    loudness = one(*pieces[0])
    for cut in pieces[1:]:
        loudness = loudness * one(*cut)
    return loudness


def different_ones(key, rows, amount, top, lift):
    order = jax.random.permutation(jax.random.fold_in(key, 1), amount)
    favour = order
    for power in range(3):
        favour = favour * favour // amount
    favour = favour * lift // amount
    chance = jax.random.randint(jax.random.fold_in(key, 2), (rows, amount), 0, 4096) + favour
    holders = jax.random.permutation(jax.random.fold_in(key, 3), rows)[jnp.arange(amount) % rows]
    chance = jnp.where(jnp.arange(rows)[:, None] == holders[None, :], 1 << 14, chance)
    score = chance * amount + jnp.arange(amount)
    return lax.top_k(score.astype(jnp.int32), top)[1].astype(jnp.int32)


def gaussian(own_key, shape, width, bound, shards=(), kind=jnp.bfloat16):
    array = width * jax.random.normal(own_key, shape, jnp.float32)
    if shards:
        array = array * block_scale(own_key, shape, shards, -0.22, 0.18)
    return jnp.clip(array, -bound, bound).astype(kind)


def setup_inputs(seed: int = 0, part: int = 0) -> dict:
    key_of = jax.random.split(jax.random.key(seed), 8)
    part_splits = jax.random.split(jax.random.fold_in(key_of[7], part), 8)
    tokens = gaussian(part_splits[0], (STEPS, ROWS, D), 1.0, 6.0, ((1, 16),))
    w_gate = gaussian(key_of[1], (E, D, FF), D ** -0.5, 0.078125, ((2, 16),))
    w_up = gaussian(key_of[2], (E, D, FF), D ** -0.5, 0.078125, ((2, 16),))
    w_down = gaussian(key_of[3], (E, FF, D), FF ** -0.5, 0.0625, ((1, 16),))
    expert_ids = different_ones(part_splits[4], STEPS * ROWS, E, TOPK, 8192).reshape((STEPS, ROWS, TOPK))
    gate_weights = jnp.clip(jax.random.uniform(part_splits[5], (STEPS, ROWS, TOPK), jnp.float32, 0.099609375, 0.8984375), 0.099609375, 0.8984375).astype(jnp.bfloat16)
    return_order = jax.vmap(lambda own: jax.random.permutation(own, ROWS))(jax.random.split(part_splits[6], STEPS)).reshape((STEPS, ROWS)).astype(jnp.int32)
    return dict(tokens=tokens, w_gate=w_gate, w_up=w_up, w_down=w_down, expert_ids=expert_ids, gate_weights=gate_weights, return_order=return_order)


def route_table(expert_ids, gate_weights, num_experts):
    labels = jnp.arange(num_experts, dtype=jnp.int32)
    chosen = expert_ids[..., None] == labels
    return jnp.sum(jnp.where(chosen, gate_weights[..., None].astype(jnp.float32), jnp.float32(0.0)), axis=-2)


def reference(tokens, w_gate, w_up, w_down, expert_ids, gate_weights, return_order):
    num_experts = w_gate.shape[0]
    routing = route_table(expert_ids, gate_weights, num_experts).reshape(STEPS * ROWS, num_experts)
    flat_rows = tokens.reshape(STEPS * ROWS, D)
    combined = jnp.zeros((STEPS * ROWS, D), jnp.float32)
    for expert in range(num_experts):
        gate_part = jnp.dot(flat_rows, w_gate[expert], preferred_element_type=jnp.float32)
        up_part = jnp.dot(flat_rows, w_up[expert], preferred_element_type=jnp.float32)
        hidden = (jax.nn.silu(gate_part) * up_part * routing[:, expert:expert + 1]).astype(jnp.bfloat16)
        combined = combined + jnp.dot(hidden, w_down[expert], preferred_element_type=jnp.float32)
    combined = combined.reshape(STEPS, ROWS, D)
    ordered = jnp.take_along_axis(combined, return_order[:, :, None], axis=1)
    return ordered.astype(jnp.bfloat16)
```

```python
import functools

import jax
import jax.numpy as jnp
from jax import lax
from jax.experimental import pallas as pl
from jax.experimental.pallas import tpu as pltpu
from jax.sharding import PartitionSpec as P

MIB = 1 << 20
ARENA = 30 * MIB
SCOPED = 24
VMEM = pl.BlockSpec(memory_space=pltpu.VMEM)
ANY = pl.BlockSpec(memory_space=pl.ANY)
BF16, F32 = jnp.bfloat16, jnp.float32


def in_vmem(x):
    return pltpu.with_memory_space_constraint(x, pltpu.VMEM)


def in_hbm(x):
    return pltpu.with_memory_space_constraint(x, pltpu.HBM)


def cost(flops, size):
    return pl.CostEstimate(flops=flops, bytes_accessed=size, transcendentals=0)


def swap(x, mask):
    n = lax.axis_size("hid")
    return lax.ppermute(x, "hid", [(i, i ^ mask) for i in range(n)])


def split_kernel(tokens_ref, *out_refs):
    steps, own, _ = tokens_ref.shape
    first = 0
    for out_ref in out_refs:
        columns = out_ref.shape[1]
        for s in range(steps):
            out_ref[s * own : (s + 1) * own] = tokens_ref[s, :, first : first + columns]
        first += columns


def split(tokens, widths):
    steps, own, _ = tokens.shape
    return pl.pallas_call(
        split_kernel,
        in_specs=[VMEM],
        out_specs=[VMEM] * len(widths),
        out_shape=[pltpu.VMEM((steps * own, w), tokens.dtype) for w in widths],
        compiler_params=pltpu.CompilerParams(vmem_limit_bytes=2 * MIB),
        cost_estimate=cost(0, 4 * tokens.size),
        name="split",
    )(in_vmem(tokens))


def stack_kernel(places, *refs):
    *part_refs, out_ref = refs[: len(places)] + refs[-1:]
    for part_ref, (column, rows) in zip(part_refs, places):
        columns = part_ref.shape[1]
        per = part_ref.shape[0] // len(rows)
        for i, row in enumerate(rows):
            out_ref[row * per : (row + 1) * per, column : column + columns] = part_ref[i * per : (i + 1) * per]


def stack(parts, places, shape, after):
    return pl.pallas_call(
        functools.partial(stack_kernel, places),
        in_specs=[VMEM] * len(parts) + [ANY],
        out_specs=VMEM,
        out_shape=pltpu.VMEM(shape, parts[0].dtype),
        compiler_params=pltpu.CompilerParams(vmem_limit_bytes=2 * MIB),
        cost_estimate=cost(0, 4 * shape[0] * shape[1]),
        name="stack",
    )(*[in_vmem(part) for part in parts], after)


def load_kernel(pieces, gate_ref, up_ref, after_ref, out_ref, token_ref, sem):
    width = gate_ref.shape[1]
    copies = []
    for i, piece in enumerate(pieces):
        source = up_ref if piece % 2 else gate_ref
        copies.append(pltpu.make_async_copy(source.at[piece // 2], out_ref.at[pl.ds(i * width, width)], sem.at[i]))
    for copy in copies:
        copy.start()
    token_ref[...] = jnp.zeros_like(token_ref)
    for copy in copies:
        copy.wait()


def load(w_gate, w_up, after, pieces):
    _, width, units = w_gate.shape
    return pl.pallas_call(
        functools.partial(load_kernel, pieces),
        in_specs=[ANY, ANY, ANY],
        out_specs=[VMEM, VMEM],
        out_shape=[pltpu.VMEM((len(pieces) * width, units), w_gate.dtype), pltpu.VMEM((8, 128), F32)],
        scratch_shapes=[pltpu.SemaphoreType.DMA((len(pieces),))],
        compiler_params=pltpu.CompilerParams(vmem_limit_bytes=2 * MIB),
        cost_estimate=cost(0, 2 * len(pieces) * width * units),
        name="load",
    )(in_hbm(w_gate), in_hbm(w_up), after)


def place_of(row, n, steps, own, me):
    per = steps * own
    slot, rest = row // per, row % per
    far = n // 4
    mask = slot // (2 * far) + 2 * ((slot // far) % 2) + 4 * (slot % far)
    return (rest // own) * (n * own) + (me ^ mask) * own + rest % own


def experts_kernel(
    n, steps, own, loads, blocks, half_ref, other_ref, table_ref, gate_ref, up_ref, down_ref, *refs
):
    refs = refs[loads:]
    (h_ref, keep_ref, send_ref), arena_refs = refs[:3], refs[3 : 3 + loads]
    x_ref, rest_ref, route, order, rest_sem, down_sem = refs[3 + loads :]
    half, width = half_ref.shape
    rows = 2 * half
    experts, units, _ = down_ref.shape
    depth = experts * units
    homes = [ref.at[pl.ds(i, width)] for ref in arena_refs for i in range(0, ref.shape[0], width)]
    count = len(homes)
    spares = [rest_ref.at[pl.ds(i, width)] for i in range(0, rest_ref.shape[0], width)]
    late = []
    for p in range(count, 2 * experts):
        at = p - count
        home = spares[at] if at < len(spares) else homes[at - len(spares)]
        source = (up_ref if p % 2 else gate_ref).at[p // 2]
        late.append((home, pltpu.make_async_copy(source, home, rest_sem.at[at])))
    taken = max(len(late) - len(spares), 0)
    for _, copy in late[:2]:
        copy.start()
    x_ref[:half] = half_ref[...]
    x_ref[half:] = other_ref[...]

    me = lax.axis_index("hid")
    shape = (rows, rows)
    down = lax.broadcasted_iota(jnp.int32, shape, 0)
    across = lax.broadcasted_iota(jnp.int32, shape, 1)
    pick = (place_of(down, n, steps, own, me) == across).astype(BF16)
    mine = jnp.dot(pick, table_ref[...].astype(BF16), preferred_element_type=F32)
    step = (lax.broadcasted_iota(jnp.int32, (rows, 1), 0) % (steps * own)) // own
    source = mine[:, 4:5].astype(jnp.int32) + step * (n * own)
    order[...] = (place_of(across, n, steps, own, me) == source).astype(BF16)
    for e in range(experts):
        route[e] = jnp.where(mine[:, 0:1] == e, mine[:, 2:3], 0.0) + jnp.where(
            mine[:, 1:2] == e, mine[:, 3:4], 0.0
        )

    fit = width // depth

    def block_home(b):
        return homes[taken + b // fit].at[pl.ds(b % fit * depth, depth)]

    def block_copies(b):
        return [
            pltpu.make_async_copy(
                down_ref.at[e, :, pl.ds(b * units, units)],
                block_home(b).at[pl.ds(e * units, units)],
                down_sem.at[b, e],
            )
            for e in range(experts)
        ]

    def piece(p):
        if p < count:
            return homes[p][...]
        home, copy = late[p - count]
        copy.wait()
        return home[...]

    begun = 0
    for e in range(experts):
        gate = jnp.dot(x_ref[...], piece(2 * e), preferred_element_type=F32)
        up = jnp.dot(x_ref[...], piece(2 * e + 1), preferred_element_type=F32)
        if e == 0:
            for _, copy in late[2:]:
                copy.start()
        free = (min(2 * (e + 1), count) - taken) * fit
        until = blocks if e == experts - 1 else min(-(-blocks * e // experts), free)
        for b in range(begun, until):
            for copy in block_copies(b):
                copy.start()
        begun = until
        hidden = gate / (1.0 + jnp.exp(-gate)) * up * route[e]
        hidden = jnp.dot(order[...], hidden.astype(BF16), preferred_element_type=F32)
        h_ref[:, e * units : (e + 1) * units] = hidden.astype(BF16)
    for b in range(blocks):
        for copy in block_copies(b):
            copy.wait()
        total = jnp.dot(h_ref[...], block_home(b)[...], preferred_element_type=F32)
        keep_ref[:, b * units : (b + 1) * units] = total[:half]
        send_ref[:, b * units : (b + 1) * units] = total[half:].astype(BF16)


def experts_of(half, other, table, w_gate, w_up, w_down, arena, blocks, n, steps, own):
    experts, units, width = w_down.shape
    rows = 2 * half.shape[0]
    columns = blocks * units
    rest = max(2 * experts - sum(buffer.shape[0] for buffer in arena) // width, 1)
    h, keep, send, *_ = pl.pallas_call(
        functools.partial(experts_kernel, n, steps, own, len(arena), blocks),
        in_specs=[VMEM] * 3 + [ANY] * 3 + [VMEM] * len(arena),
        out_specs=[VMEM] * (3 + len(arena)),
        out_shape=[
            pltpu.VMEM((rows, experts * units), BF16),
            pltpu.VMEM((rows // 2, columns), F32),
            pltpu.VMEM((rows // 2, columns), BF16),
        ]
        + [pltpu.VMEM(buffer.shape, buffer.dtype) for buffer in arena],
        scratch_shapes=[
            pltpu.VMEM((rows, width), BF16),
            pltpu.VMEM((max(rest - 1, 1) * width, units), BF16),
            pltpu.VMEM((experts, rows, 1), F32),
            pltpu.VMEM((rows, rows), BF16),
            pltpu.SemaphoreType.DMA((rest,)),
            pltpu.SemaphoreType.DMA((blocks, experts)),
        ],
        input_output_aliases={6 + i: 3 + i for i in range(len(arena))},
        compiler_params=pltpu.CompilerParams(vmem_limit_bytes=SCOPED * MIB),
        cost_estimate=cost(6 * rows * w_down.size, 2 * w_down.size),
        name="experts",
    )(
        in_vmem(half), in_vmem(other), in_vmem(table), in_hbm(w_gate), in_hbm(w_up), in_hbm(w_down),
        *[in_vmem(buffer) for buffer in arena],
    )
    return h, keep, send


def down_kernel(first, h_ref, down_ref, keep_ref, send_ref, w_ref, sem):
    half = keep_ref.shape[0]
    experts, units, _ = down_ref.shape
    blocks = w_ref.shape[0]
    copies = [
        [
            pltpu.make_async_copy(
                down_ref.at[e, :, pl.ds((first + b) * units, units)], w_ref.at[b, pl.ds(e * units, units)], sem.at[b, e]
            )
            for e in range(experts)
        ]
        for b in range(blocks)
    ]
    for block in copies:
        for copy in block:
            copy.start()
    for b, block in enumerate(copies):
        for copy in block:
            copy.wait()
        total = jnp.dot(h_ref[...], w_ref[b], preferred_element_type=F32)
        keep_ref[:, b * units : (b + 1) * units] = total[:half]
        send_ref[:, b * units : (b + 1) * units] = total[half:].astype(BF16)


def down(h, w_down, first, blocks):
    experts, units, _ = w_down.shape
    rows, depth = h.shape
    half, columns = rows // 2, blocks * units
    return pl.pallas_call(
        functools.partial(down_kernel, first),
        in_specs=[VMEM, ANY],
        out_specs=[VMEM] * 2,
        out_shape=[pltpu.VMEM((half, columns), F32), pltpu.VMEM((half, columns), BF16)],
        scratch_shapes=[pltpu.VMEM((blocks, depth, units), BF16), pltpu.SemaphoreType.DMA((blocks, experts))],
        compiler_params=pltpu.CompilerParams(vmem_limit_bytes=16 * MIB),
        cost_estimate=cost(2 * rows * depth * columns, 2 * depth * columns),
        name="down",
    )(in_vmem(h), in_hbm(w_down))


def add_kernel(groups, keep_ref, got_ref, *out_refs):
    count = sum(len(group) for group in groups)
    per = keep_ref.shape[0] // count
    for group, out_ref in zip(groups, out_refs):
        for i, block in enumerate(group):
            rows = slice(block * per, (block + 1) * per)
            total = keep_ref[rows] + got_ref[rows].astype(F32)
            out_ref[i * per : (i + 1) * per] = total.astype(out_ref.dtype)


def add(keep, got, groups):
    per = keep.shape[0] // sum(len(group) for group in groups)
    columns = keep.shape[1]
    return pl.pallas_call(
        functools.partial(add_kernel, groups),
        in_specs=[VMEM, VMEM],
        out_specs=[VMEM] * len(groups),
        out_shape=[pltpu.VMEM((per * len(g), columns), BF16 if i else F32) for i, g in enumerate(groups)],
        compiler_params=pltpu.CompilerParams(vmem_limit_bytes=2 * MIB),
        cost_estimate=cost(0, 8 * keep.size),
        name="add",
    )(in_vmem(keep), in_vmem(got))


def sum_kernel(far, *refs):
    *part_refs, out_ref = refs
    first = 0
    steps, own, _ = out_ref.shape
    for keep_ref, got_refs in ((part_refs[0], part_refs[1:far]), (part_refs[far], part_refs[far + 1 :])):
        total = keep_ref[...]
        for got_ref in got_refs:
            total = total + got_ref[...].astype(F32)
        total = total.astype(out_ref.dtype)
        columns = keep_ref.shape[1]
        for s in range(steps):
            out_ref[s, :, first : first + columns] = total[s * own : (s + 1) * own]
        first += columns


def body(tokens, w_gate, w_up, w_down, expert_ids, gate_weights, return_order):
    steps, own, width = tokens.shape
    experts, _, units = w_gate.shape
    n = lax.axis_size("hid")
    far = n // 4
    per = steps * own
    rows = per * n
    table = jnp.concatenate(
        [expert_ids.astype(F32), gate_weights.astype(F32), return_order[..., None].astype(F32)], axis=-1
    ).reshape(rows, 5)

    blocks = width // units
    lead = (2 * blocks + 2) // 3
    a = lead * units
    b = width - a
    count = min(2 * experts, ARENA // (2 * width * units))
    cuts = [count // 4, 3 * count // 4, count]
    pieces = [range(0, cuts[0]), range(cuts[0], cuts[1]), range(cuts[1], cuts[2])]
    xa, xb = split(tokens, [a, b])
    za = [swap(xa, 4 * z) for z in range(1, far)]
    yb = swap(xb, 2)
    arena0, ready = load(w_gate, w_up, table, pieces[0])
    xb = stack([xb, yb], [(0, [0]), (0, [1])], (2 * per, b), ready)
    zb = [swap(xb, 4 * z) for z in range(1, far)]
    arena1, ready = load(w_gate, w_up, xb, pieces[1])
    xa = stack([xa] + za, [(0, [z]) for z in range(far)], (far * per, a), ready)
    ya = swap(xa, 2)
    arena2, ready = load(w_gate, w_up, xa, pieces[2])
    half = stack(
        [xa, ya, xb] + zb,
        [(0, [0]), (0, [1])] + [(a, [z, far + z]) for z in range(far)],
        (2 * far * per, width),
        ready,
    )
    other = swap(half, 1)
    h, keep_a, send_a = experts_of(half, other, table, w_gate, w_up, w_down, [arena0, arena1, arena2], lead, n, steps, own)
    got_a = swap(send_a, 1)
    keep_b, send_b = down(h, w_down, lead, blocks - lead)
    got_b = swap(send_b, 1)
    keep_a, send_a = add(keep_a, got_a, [list(range(far)), list(range(far, 2 * far))])
    got_a = swap(send_a, 2)
    keep_b, *send_b = add(keep_b, got_b, [[z, far + z] for z in range(far)])
    got_b = [swap(send, 4 * (z + 1)) for z, send in enumerate(send_b)]
    keep_a, *send_a = add(keep_a, got_a, [[z] for z in range(far)])
    got_a = [swap(send, 4 * (z + 1)) for z, send in enumerate(send_a)]
    total_b = keep_b
    for got in got_b:
        total_b = total_b + got.astype(F32)
    keep_b, send_b = total_b[:per], total_b[per:].astype(BF16)
    parts = [keep_a, *got_a, keep_b, swap(send_b, 2)]
    return pl.pallas_call(
        functools.partial(sum_kernel, far),
        in_specs=[VMEM] * len(parts),
        out_specs=VMEM,
        out_shape=jax.ShapeDtypeStruct(tokens.shape, tokens.dtype),
        compiler_params=pltpu.CompilerParams(vmem_limit_bytes=4 * MIB),
        cost_estimate=cost(0, 4 * tokens.size),
        name="sum",
    )(*[in_vmem(part) for part in parts])


def solution(mesh):
    in_specs = (
        P("groups", "hid", None),
        P(None, None, "hid"),
        P(None, None, "hid"),
        P(None, "hid", None),
        P("groups", None, None),
        P("groups", None, None),
        P("groups", None),
    )
    out_specs = P("groups", "hid", None)
    return jax.shard_map(body, mesh=mesh, in_specs=in_specs, out_specs=out_specs, check_vma=False)
```

```python
import functools

import jax
import jax.numpy as jnp
from jax import lax
from jax.experimental import pallas as pl
from jax.experimental.pallas import tpu as pltpu
from jax.sharding import PartitionSpec as P

MIB = 1 << 20
SCOPED = 18
VMEM = pl.BlockSpec(memory_space=pltpu.VMEM)
ANY = pl.BlockSpec(memory_space=pl.ANY)
BF16, F32 = jnp.bfloat16, jnp.float32


def in_vmem(x):
    return pltpu.with_memory_space_constraint(x, pltpu.VMEM)


def in_hbm(x):
    return pltpu.with_memory_space_constraint(x, pltpu.HBM)


def cost(flops, size):
    return pl.CostEstimate(flops=flops, bytes_accessed=size, transcendentals=0)


def swap(x, mask):
    n = lax.axis_size("hid")
    return lax.ppermute(x, "hid", [(i, i ^ mask) for i in range(n)])


def split_kernel(tokens_ref, *out_refs):
    steps, own, _ = tokens_ref.shape
    first = 0
    for out_ref in out_refs:
        columns = out_ref.shape[1]
        for s in range(steps):
            out_ref[s * own : (s + 1) * own] = tokens_ref[s, :, first : first + columns]
        first += columns


def split(tokens, widths):
    steps, own, _ = tokens.shape
    return pl.pallas_call(
        split_kernel,
        in_specs=[VMEM],
        out_specs=[VMEM] * len(widths),
        out_shape=[pltpu.VMEM((steps * own, w), tokens.dtype) for w in widths],
        compiler_params=pltpu.CompilerParams(vmem_limit_bytes=2 * MIB),
        cost_estimate=cost(0, 4 * tokens.size),
        name="split",
    )(in_vmem(tokens))


def stack_kernel(places, *refs):
    *part_refs, out_ref = refs[: len(places)] + refs[-1:]
    for part_ref, (column, rows) in zip(part_refs, places):
        columns = part_ref.shape[1]
        per = part_ref.shape[0] // len(rows)
        for i, row in enumerate(rows):
            out_ref[row * per : (row + 1) * per, column : column + columns] = part_ref[i * per : (i + 1) * per]


def stack(parts, places, shape, after):
    return pl.pallas_call(
        functools.partial(stack_kernel, places),
        in_specs=[VMEM] * len(parts) + [ANY],
        out_specs=VMEM,
        out_shape=pltpu.VMEM(shape, parts[0].dtype),
        compiler_params=pltpu.CompilerParams(vmem_limit_bytes=2 * MIB),
        cost_estimate=cost(0, 4 * shape[0] * shape[1]),
        name="stack",
    )(*[in_vmem(part) for part in parts], after)


def load_kernel(w_ref, after_ref, out_ref, token_ref, sem):
    copy = pltpu.make_async_copy(w_ref.at[0], out_ref, sem)
    copy.start()
    token_ref[...] = jnp.zeros_like(token_ref)
    copy.wait()


def load(w, after):
    return pl.pallas_call(
        load_kernel,
        in_specs=[ANY, ANY],
        out_specs=[VMEM, VMEM],
        out_shape=[pltpu.VMEM(w.shape[1:], w.dtype), pltpu.VMEM((8, 128), F32)],
        scratch_shapes=[pltpu.SemaphoreType.DMA],
        compiler_params=pltpu.CompilerParams(vmem_limit_bytes=2 * MIB),
        cost_estimate=cost(0, 2 * w.size // w.shape[0]),
        name="load",
    )(in_hbm(w), after)


def place_of(row, n, steps, own, me):
    per = steps * own
    slot, rest = row // per, row % per
    far = n // 4
    mask = slot // (2 * far) + 2 * ((slot // far) % 2) + 4 * (slot % far)
    return (rest // own) * (n * own) + (me ^ mask) * own + rest % own


def plan_kernel(n, own, ids_ref, weights_ref, return_ref, after_ref, route_ref, order_ref):
    steps, total = return_ref.shape
    rows = steps * total
    me = lax.axis_index("hid")
    down = lax.broadcasted_iota(jnp.int32, (rows, total), 0)
    place = place_of(down, n, steps, own, me)
    across = lax.broadcasted_iota(jnp.int32, (rows, total), 1)
    picked = [jnp.zeros((rows, total), F32)] * 5
    for s in range(steps):
        here = place == across + s * total
        values = [ids_ref[s, 0:1], ids_ref[s, 1:2], weights_ref[s, 0:1], weights_ref[s, 1:2], return_ref[s : s + 1]]
        picked = [jnp.where(here, value.astype(F32), old) for value, old in zip(values, picked)]
    first, second, first_weight, second_weight, source = [jnp.sum(p, axis=1, keepdims=True) for p in picked]
    for e in range(route_ref.shape[0]):
        route_ref[e] = jnp.where(first == e, first_weight, 0.0) + jnp.where(second == e, second_weight, 0.0)
    shape = (rows, rows)
    step = (lax.broadcasted_iota(jnp.int32, (rows, 1), 0) % (steps * own)) // own
    across = lax.broadcasted_iota(jnp.int32, shape, 1)
    order_ref[...] = (place_of(across, n, steps, own, me) == source.astype(jnp.int32) + step * total).astype(BF16)


def plan(expert_ids, gate_weights, return_order, experts, n, own, after):
    steps, total = return_order.shape
    rows = steps * total
    return pl.pallas_call(
        functools.partial(plan_kernel, n, own),
        in_specs=[VMEM] * 3 + [ANY],
        out_specs=[VMEM, VMEM],
        out_shape=[pltpu.VMEM((experts, rows, 1), F32), pltpu.VMEM((rows, rows), BF16)],
        compiler_params=pltpu.CompilerParams(vmem_limit_bytes=8 * MIB),
        cost_estimate=cost(0, 4 * rows * rows),
        name="plan",
    )(jnp.swapaxes(expert_ids, 1, 2), jnp.swapaxes(gate_weights, 1, 2), return_order, after)


def experts_kernel(
    blocks, half_ref, other_ref, route_ref, order_ref, gate_ref, up_ref, down_ref, old_ref,
    h_ref, keep_ref, send_ref, first_ref, x_ref, up_buf, up_sem, down_sem,
):
    half, width = half_ref.shape
    experts, units, _ = down_ref.shape
    depth = experts * units
    up_homes = [first_ref] + [up_buf.at[e % 2] for e in range(1, experts - 1)] + [first_ref]
    up_copies = [None] + [pltpu.make_async_copy(up_ref.at[e], up_homes[e], up_sem.at[e]) for e in range(1, experts)]
    fit = width // depth
    homes = [ref.at[pl.ds(at * experts, experts)] for ref in (up_buf.at[1], up_buf.at[0], first_ref) for at in range(fit)]

    def block_copy(b):
        return pltpu.make_async_copy(down_ref.at[:, :, pl.ds(b * units, units)], homes[b], down_sem.at[b])

    def start_blocks(first, last):
        for b in range(first, min(last, blocks)):
            block_copy(b).start()

    for copy in up_copies[1:3]:
        copy.start()
    x_ref[:half] = half_ref[...]
    x_ref[half:] = other_ref[...]
    for e in range(experts):
        gate = jnp.dot(x_ref[...], gate_ref[e], preferred_element_type=F32)
        if e:
            up_copies[e].wait()
        up = jnp.dot(x_ref[...], up_homes[e].reshape(width, units)[...], preferred_element_type=F32)
        if e == 0:
            for copy in up_copies[3:]:
                copy.start()
        elif e == 1:
            start_blocks(0, fit)
        elif e == 2:
            start_blocks(fit, 2 * fit)
        else:
            start_blocks(2 * fit, blocks)
        hidden = gate / (1.0 + jnp.exp(-gate)) * up * route_ref[e]
        hidden = jnp.dot(order_ref[...], hidden.astype(BF16), preferred_element_type=F32)
        h_ref[:, e * units : (e + 1) * units] = hidden.astype(BF16)
    for b in range(blocks):
        block_copy(b).wait()
        total = jnp.dot(h_ref[...], homes[b].reshape(depth, units)[...], preferred_element_type=F32)
        keep_ref[:, b * units : (b + 1) * units] = total[:half]
        send_ref[:, b * units : (b + 1) * units] = total[half:].astype(BF16)


def experts_of(half, other, route, order, w_gate, w_up, w_down, first_up, blocks):
    experts, units, width = w_down.shape
    rows = 2 * half.shape[0]
    columns = blocks * units
    depth = experts * units
    h, keep, send, _ = pl.pallas_call(
        functools.partial(experts_kernel, blocks),
        in_specs=[VMEM] * 5 + [ANY] * 2 + [VMEM],
        out_specs=[VMEM] * 4,
        out_shape=[
            pltpu.VMEM((rows, depth), BF16),
            pltpu.VMEM((rows // 2, columns), F32),
            pltpu.VMEM((rows // 2, columns), BF16),
            pltpu.VMEM(first_up.shape, first_up.dtype),
        ],
        scratch_shapes=[
            pltpu.VMEM((rows, width), BF16),
            pltpu.VMEM((2, width // units, units, units), BF16),
            pltpu.SemaphoreType.DMA((experts,)),
            pltpu.SemaphoreType.DMA((blocks,)),
        ],
        input_output_aliases={7: 3},
        compiler_params=pltpu.CompilerParams(vmem_limit_bytes=SCOPED * MIB),
        cost_estimate=cost(0, 8 * w_down.size),
        name="experts",
    )(
        in_vmem(half), in_vmem(other), in_vmem(route), in_vmem(order),
        in_vmem(w_gate), in_hbm(w_up), in_hbm(w_down), in_vmem(first_up),
    )
    return h, keep, send


def down_kernel(first, h_ref, down_ref, keep_ref, send_ref, w_ref, sem):
    half = keep_ref.shape[0]
    experts, units, _ = down_ref.shape
    blocks = w_ref.shape[0]
    copies = [
        [
            pltpu.make_async_copy(
                down_ref.at[e, :, pl.ds((first + b) * units, units)], w_ref.at[b, pl.ds(e * units, units)], sem.at[b, e]
            )
            for e in range(experts)
        ]
        for b in range(blocks)
    ]
    for block in copies:
        for copy in block:
            copy.start()
    for b, block in enumerate(copies):
        for copy in block:
            copy.wait()
        total = jnp.dot(h_ref[...], w_ref[b], preferred_element_type=F32)
        keep_ref[:, b * units : (b + 1) * units] = total[:half]
        send_ref[:, b * units : (b + 1) * units] = total[half:].astype(BF16)


def down(h, w_down, first, blocks):
    experts, units, _ = w_down.shape
    rows, depth = h.shape
    half, columns = rows // 2, blocks * units
    return pl.pallas_call(
        functools.partial(down_kernel, first),
        in_specs=[VMEM, ANY],
        out_specs=[VMEM] * 2,
        out_shape=[pltpu.VMEM((half, columns), F32), pltpu.VMEM((half, columns), BF16)],
        scratch_shapes=[pltpu.VMEM((blocks, depth, units), BF16), pltpu.SemaphoreType.DMA((blocks, experts))],
        compiler_params=pltpu.CompilerParams(vmem_limit_bytes=16 * MIB),
        cost_estimate=cost(2 * rows * depth * columns, 2 * depth * columns),
        name="down",
    )(in_vmem(h), in_hbm(w_down))


def add_kernel(groups, keep_ref, got_ref, *out_refs):
    count = sum(len(group) for group in groups)
    per = keep_ref.shape[0] // count
    for group, out_ref in zip(groups, out_refs):
        for i, block in enumerate(group):
            rows = slice(block * per, (block + 1) * per)
            total = keep_ref[rows] + got_ref[rows].astype(F32)
            out_ref[i * per : (i + 1) * per] = total.astype(out_ref.dtype)


def add(keep, got, groups):
    per = keep.shape[0] // sum(len(group) for group in groups)
    columns = keep.shape[1]
    return pl.pallas_call(
        functools.partial(add_kernel, groups),
        in_specs=[VMEM, VMEM],
        out_specs=[VMEM] * len(groups),
        out_shape=[pltpu.VMEM((per * len(g), columns), BF16 if i else F32) for i, g in enumerate(groups)],
        compiler_params=pltpu.CompilerParams(vmem_limit_bytes=2 * MIB),
        cost_estimate=cost(0, 8 * keep.size),
        name="add",
    )(in_vmem(keep), in_vmem(got))


def sum_kernel(far, *refs):
    *part_refs, out_ref = refs
    first = 0
    steps, own, _ = out_ref.shape
    for keep_ref, got_refs in ((part_refs[0], part_refs[1:far]), (part_refs[far], part_refs[far + 1 :])):
        total = keep_ref[...]
        for got_ref in got_refs:
            total = total + got_ref[...].astype(F32)
        total = total.astype(out_ref.dtype)
        columns = keep_ref.shape[1]
        for s in range(steps):
            out_ref[s, :, first : first + columns] = total[s * own : (s + 1) * own]
        first += columns


def body(tokens, w_gate, w_up, w_down, expert_ids, gate_weights, return_order):
    steps, own, width = tokens.shape
    experts, _, units = w_gate.shape
    n = lax.axis_size("hid")
    far = n // 4
    per = steps * own
    rows = per * n
    blocks = width // units
    lead = (2 * blocks + 2) // 3
    a = lead * units
    b = width - a
    xa, xb = split(tokens, [a, b])
    za = [swap(xa, 4 * z) for z in range(1, far)]
    yb = swap(xb, 2)
    w_up = w_up.reshape(experts, blocks, units, units)
    first_up, ready = load(w_up, xa)
    xb = stack([xb, yb], [(0, [0]), (0, [1])], (2 * per, b), ready)
    zb = [swap(xb, 4 * z) for z in range(1, far)]
    xa = stack([xa] + za, [(0, [z]) for z in range(far)], (far * per, a), xb)
    ya = swap(xa, 2)
    route, order = plan(expert_ids, gate_weights, return_order, experts, n, own, xa)
    half = stack(
        [xa, ya, xb] + zb,
        [(0, [0]), (0, [1])] + [(a, [z, far + z]) for z in range(far)],
        (2 * far * per, width),
        order,
    )
    other = swap(half, 1)
    h, keep_a, send_a = experts_of(half, other, route, order, w_gate, w_up, w_down, first_up, lead)
    got_a = swap(send_a, 1)
    keep_b, send_b = down(h, w_down, lead, blocks - lead)
    got_b = swap(send_b, 1)
    keep_a, send_a = add(keep_a, got_a, [list(range(far)), list(range(far, 2 * far))])
    got_a = swap(send_a, 2)
    keep_b, *send_b = add(keep_b, got_b, [[z, far + z] for z in range(far)])
    got_b = [swap(send, 4 * (z + 1)) for z, send in enumerate(send_b)]
    keep_a, *send_a = add(keep_a, got_a, [[z] for z in range(far)])
    got_a = [swap(send, 4 * (z + 1)) for z, send in enumerate(send_a)]
    total_b = keep_b
    for got in got_b:
        total_b = total_b + got.astype(F32)
    keep_b, send_b = total_b[:per], total_b[per:].astype(BF16)
    parts = [keep_a, *got_a, keep_b, swap(send_b, 2)]
    return pl.pallas_call(
        functools.partial(sum_kernel, far),
        in_specs=[VMEM] * len(parts),
        out_specs=VMEM,
        out_shape=jax.ShapeDtypeStruct(tokens.shape, tokens.dtype),
        compiler_params=pltpu.CompilerParams(vmem_limit_bytes=4 * MIB),
        cost_estimate=cost(0, 4 * tokens.size),
        name="sum",
    )(*[in_vmem(part) for part in parts])


def solution(mesh):
    in_specs = (
        P("groups", "hid", None),
        P(None, None, "hid"),
        P(None, None, "hid"),
        P(None, "hid", None),
        P("groups", None, None),
        P("groups", None, None),
        P("groups", None),
    )
    out_specs = P("groups", "hid", None)
    return jax.shard_map(body, mesh=mesh, in_specs=in_specs, out_specs=out_specs, check_vma=False)
```

```python
import functools

import jax
import jax.numpy as jnp
from jax import lax
from jax.experimental import pallas as pl
from jax.experimental.pallas import tpu as pltpu
from jax.sharding import PartitionSpec as P

MIB = 1 << 20
SCOPED = 10
VMEM = pl.BlockSpec(memory_space=pltpu.VMEM)
ANY = pl.BlockSpec(memory_space=pl.ANY)
BF16, F32 = jnp.bfloat16, jnp.float32


def in_vmem(x):
    return pltpu.with_memory_space_constraint(x, pltpu.VMEM)


def in_hbm(x):
    return pltpu.with_memory_space_constraint(x, pltpu.HBM)


def cost(flops, size):
    return pl.CostEstimate(flops=flops, bytes_accessed=size, transcendentals=0)


def swap(x, mask):
    n = lax.axis_size("hid")
    return lax.ppermute(x, "hid", [(i, i ^ mask) for i in range(n)])


def split_kernel(tokens_ref, *out_refs):
    steps, own, _ = tokens_ref.shape
    first = 0
    for out_ref in out_refs:
        columns = out_ref.shape[1]
        for s in range(steps):
            out_ref[s * own : (s + 1) * own] = tokens_ref[s, :, first : first + columns]
        first += columns


def split(tokens, widths):
    steps, own, _ = tokens.shape
    return pl.pallas_call(
        split_kernel,
        in_specs=[VMEM],
        out_specs=[VMEM] * len(widths),
        out_shape=[pltpu.VMEM((steps * own, w), tokens.dtype) for w in widths],
        compiler_params=pltpu.CompilerParams(vmem_limit_bytes=2 * MIB),
        cost_estimate=cost(0, 4 * tokens.size),
        name="split",
    )(in_vmem(tokens))


def stack_kernel(places, *refs):
    *part_refs, out_ref = refs[: len(places)] + refs[-1:]
    for part_ref, (column, rows) in zip(part_refs, places):
        columns = part_ref.shape[1]
        per = part_ref.shape[0] // len(rows)
        for i, row in enumerate(rows):
            out_ref[row * per : (row + 1) * per, column : column + columns] = part_ref[i * per : (i + 1) * per]


def stack(parts, places, shape, after):
    return pl.pallas_call(
        functools.partial(stack_kernel, places),
        in_specs=[VMEM] * len(parts) + [ANY],
        out_specs=VMEM,
        out_shape=pltpu.VMEM(shape, parts[0].dtype),
        compiler_params=pltpu.CompilerParams(vmem_limit_bytes=2 * MIB),
        cost_estimate=cost(0, 4 * shape[0] * shape[1]),
        name="stack",
    )(*[in_vmem(part) for part in parts], after)


def load_kernel(e, w_ref, after_ref, out_ref, token_ref, sem):
    copy = pltpu.make_async_copy(w_ref.at[e], out_ref, sem)
    copy.start()
    token_ref[...] = jnp.zeros_like(token_ref)
    copy.wait()


def load(w, e, after):
    return pl.pallas_call(
        functools.partial(load_kernel, e),
        in_specs=[ANY, ANY],
        out_specs=[VMEM, VMEM],
        out_shape=[pltpu.VMEM(w.shape[1:], w.dtype), pltpu.VMEM((8, 128), F32)],
        scratch_shapes=[pltpu.SemaphoreType.DMA],
        compiler_params=pltpu.CompilerParams(vmem_limit_bytes=2 * MIB),
        cost_estimate=cost(0, 2 * w.size // w.shape[0]),
        name="load",
    )(in_hbm(w), after)


def place_of(row, n, steps, own, me):
    per = steps * own
    slot, rest = row // per, row % per
    far = n // 4
    mask = slot // (2 * far) + 2 * ((slot // far) % 2) + 4 * (slot % far)
    return (rest // own) * (n * own) + (me ^ mask) * own + rest % own


def plan_kernel(n, own, ids_ref, weights_ref, return_ref, after_ref, route_ref, order_ref):
    steps, total = return_ref.shape
    rows = steps * total
    me = lax.axis_index("hid")
    down = lax.broadcasted_iota(jnp.int32, (rows, total), 0)
    place = place_of(down, n, steps, own, me)
    across = lax.broadcasted_iota(jnp.int32, (rows, total), 1)
    picked = [jnp.zeros((rows, total), F32)] * 5
    for s in range(steps):
        here = place == across + s * total
        values = [ids_ref[s, 0:1], ids_ref[s, 1:2], weights_ref[s, 0:1], weights_ref[s, 1:2], return_ref[s : s + 1]]
        picked = [jnp.where(here, value.astype(F32), old) for value, old in zip(values, picked)]
    first, second, first_weight, second_weight, source = [jnp.sum(p, axis=1, keepdims=True) for p in picked]
    for e in range(route_ref.shape[0]):
        route_ref[e] = jnp.where(first == e, first_weight, 0.0) + jnp.where(second == e, second_weight, 0.0)
    shape = (rows, rows)
    step = (lax.broadcasted_iota(jnp.int32, (rows, 1), 0) % (steps * own)) // own
    across = lax.broadcasted_iota(jnp.int32, shape, 1)
    order_ref[...] = (place_of(across, n, steps, own, me) == source.astype(jnp.int32) + step * total).astype(BF16)


def plan(expert_ids, gate_weights, return_order, experts, n, own, after):
    steps, total = return_order.shape
    rows = steps * total
    return pl.pallas_call(
        functools.partial(plan_kernel, n, own),
        in_specs=[VMEM] * 3 + [ANY],
        out_specs=[VMEM, VMEM],
        out_shape=[pltpu.VMEM((experts, rows, 1), F32), pltpu.VMEM((rows, rows), BF16)],
        compiler_params=pltpu.CompilerParams(vmem_limit_bytes=8 * MIB),
        cost_estimate=cost(0, 4 * rows * rows),
        name="plan",
    )(jnp.swapaxes(expert_ids, 1, 2), jnp.swapaxes(gate_weights, 1, 2), return_order, after)


def experts_kernel(
    half_ref, other_ref, route_ref, order_ref, gate_ref, up_ref, down_ref, *refs
):
    early = len(refs) // 2 - 3
    keep_ref, send_ref = refs[early : early + 2]
    homes = list(refs[early + 2 : 2 * early + 2])
    x_ref, h_ref, up_buf, up_sem, down_sem = refs[2 * early + 2 :]
    half, width = half_ref.shape
    experts, units, _ = down_ref.shape
    depth = experts * units
    blocks = width // units
    fit = width // depth
    homes.append(up_buf)
    homes += homes[: experts - early - 1]
    up_copies = {e: pltpu.make_async_copy(up_ref.at[e], homes[e], up_sem.at[e]) for e in range(early, experts)}
    down_homes = homes[experts - early - 1 : experts]
    down_homes = [ref.at[pl.ds(i * experts, experts)] for ref in down_homes for i in range(fit)]
    slots = len(down_homes)

    def block_copy(b):
        return pltpu.make_async_copy(
            down_ref.at[:, :, pl.ds(b * units, units)], down_homes[b % slots], down_sem.at[b % slots]
        )

    def start_blocks(first, last):
        for b in range(first, min(last, blocks)):
            block_copy(b).start()

    up_copies[early].start()
    x_ref[:half] = half_ref[...]
    x_ref[half:] = other_ref[...]
    for e in range(experts):
        gate = jnp.dot(x_ref[...], gate_ref[e], preferred_element_type=F32)
        if e in up_copies:
            up_copies[e].wait()
        up = jnp.dot(x_ref[...], homes[e].reshape(width, units)[...], preferred_element_type=F32)
        if e + early + 1 < experts:
            up_copies[e + early + 1].start()
        else:
            first = (e + early + 1 - experts) * fit
            start_blocks(first, min(first + fit, slots))
        hidden = gate / (1.0 + jnp.exp(-gate)) * up * route_ref[e]
        hidden = jnp.dot(order_ref[...], hidden.astype(BF16), preferred_element_type=F32)
        h_ref[:, e * units : (e + 1) * units] = hidden.astype(BF16)
    for b in range(blocks):
        block_copy(b).wait()
        w = down_homes[b % slots].reshape(depth, units)
        total = jnp.dot(h_ref[...], w[...], preferred_element_type=F32)
        start_blocks(b + slots, b + slots + 1)
        keep_ref[:, b * units : (b + 1) * units] = total[:half]
        send_ref[:, b * units : (b + 1) * units] = total[half:].astype(BF16)


def experts_of(half, other, route, order, w_gate, w_up, w_down, early):
    experts, units, width = w_down.shape
    rows = 2 * half.shape[0]
    keep, send, *_ = pl.pallas_call(
        experts_kernel,
        in_specs=[VMEM] * 5 + [ANY] * 2 + [VMEM] * len(early),
        out_specs=[VMEM] * (2 + len(early)),
        out_shape=[pltpu.VMEM((rows // 2, width), F32), pltpu.VMEM((rows // 2, width), BF16)]
        + [pltpu.VMEM(w.shape, w.dtype) for w in early],
        scratch_shapes=[
            pltpu.VMEM((rows, width), BF16),
            pltpu.VMEM((rows, experts * units), BF16),
            pltpu.VMEM(early[0].shape, BF16),
            pltpu.SemaphoreType.DMA((experts,)),
            pltpu.SemaphoreType.DMA((width // units,)),
        ],
        input_output_aliases={7 + i: 2 + i for i in range(len(early))},
        compiler_params=pltpu.CompilerParams(vmem_limit_bytes=SCOPED * MIB),
        cost_estimate=cost(0, 8 * w_down.size),
        name="experts",
    )(
        in_vmem(half), in_vmem(other), in_vmem(route), in_vmem(order), in_vmem(w_gate), in_hbm(w_up), in_hbm(w_down),
        *[in_vmem(w) for w in early],
    )
    return keep, send


def add_kernel(first, groups, keep_ref, *refs):
    got_refs, out_refs = refs[: -len(groups)], refs[-len(groups) :]
    per = out_refs[0].shape[0] // len(groups[0])
    columns = slice(first, first + out_refs[0].shape[1])
    for group, out_ref in zip(groups, out_refs):
        for i, block in enumerate(group):
            rows = slice(block * per, (block + 1) * per)
            total = keep_ref[rows, columns]
            for got_ref in got_refs:
                total = total + got_ref[rows, columns].astype(F32)
            out_ref[i * per : (i + 1) * per] = total.astype(out_ref.dtype)


def add(keep, gots, first, columns, groups):
    per = keep.shape[0] // sum(len(group) for group in groups)
    return pl.pallas_call(
        functools.partial(add_kernel, first, groups),
        in_specs=[VMEM] * (1 + len(gots)),
        out_specs=[VMEM] * len(groups),
        out_shape=[pltpu.VMEM((per * len(g), columns), BF16 if i else F32) for i, g in enumerate(groups)],
        compiler_params=pltpu.CompilerParams(vmem_limit_bytes=2 * MIB),
        cost_estimate=cost(0, 8 * keep.shape[0] * columns),
        name="add",
    )(in_vmem(keep), *[in_vmem(got) for got in gots])


def sum_kernel(far, *refs):
    *part_refs, out_ref = refs
    first = 0
    steps, own, _ = out_ref.shape
    for keep_ref, got_refs in ((part_refs[0], part_refs[1:far]), (part_refs[far], part_refs[far + 1 :])):
        total = keep_ref[...]
        for got_ref in got_refs:
            total = total + got_ref[...].astype(F32)
        total = total.astype(out_ref.dtype)
        columns = keep_ref.shape[1]
        for s in range(steps):
            out_ref[s, :, first : first + columns] = total[s * own : (s + 1) * own]
        first += columns


def body(tokens, w_gate, w_up, w_down, expert_ids, gate_weights, return_order):
    steps, own, width = tokens.shape
    experts, _, units = w_gate.shape
    n = lax.axis_size("hid")
    far = n // 4
    per = steps * own
    rows = per * n
    blocks = width // units
    lead = (2 * blocks + 2) // 3
    a = lead * units
    b = width - a
    xa, xb = split(tokens, [a, b])
    za = [swap(xa, 4 * z) for z in range(1, far)]
    yb = swap(xb, 2)
    w_up = w_up.reshape(experts, blocks, units, units)
    up0, ready = load(w_up, 0, xa)
    xb = stack([xb, yb], [(0, [0]), (0, [1])], (2 * per, b), ready)
    zb = [swap(xb, 4 * z) for z in range(1, far)]
    xa = stack([xa] + za, [(0, [z]) for z in range(far)], (far * per, a), xb)
    ya = swap(xa, 2)
    up1, ready = load(w_up, 1, xa)
    route, order = plan(expert_ids, gate_weights, return_order, experts, n, own, ready)
    half = stack(
        [xa, ya, xb] + zb,
        [(0, [0]), (0, [1])] + [(a, [z, far + z]) for z in range(far)],
        (2 * far * per, width),
        order,
    )
    other = swap(half, 1)
    keep, send = experts_of(half, other, route, order, w_gate, w_up, w_down, [up0, up1])

    got = swap(send, 1)
    keep_a, send_a = add(keep, [got], 0, a, [list(range(far)), list(range(far, 2 * far))])
    got_a = swap(send_a, 2)
    keep_b, *send_b = add(keep, [got], a, b, [[z, far + z] for z in range(far)])
    got_b = [swap(send, 4 * (z + 1)) for z, send in enumerate(send_b)]
    keep_a, *send_a = add(keep_a, [got_a], 0, a, [[z] for z in range(far)])
    got_a = [swap(send, 4 * (z + 1)) for z, send in enumerate(send_a)]
    keep_b, send_b = add(keep_b, got_b, 0, b, [[0], [1]])
    parts = [keep_a, *got_a, keep_b, swap(send_b, 2)]
    return pl.pallas_call(
        functools.partial(sum_kernel, far),
        in_specs=[VMEM] * len(parts),
        out_specs=VMEM,
        out_shape=jax.ShapeDtypeStruct(tokens.shape, tokens.dtype),
        compiler_params=pltpu.CompilerParams(vmem_limit_bytes=4 * MIB),
        cost_estimate=cost(0, 4 * tokens.size),
        name="sum",
    )(*[in_vmem(part) for part in parts])


def solution(mesh):
    in_specs = (
        P("groups", "hid", None),
        P(None, None, "hid"),
        P(None, None, "hid"),
        P(None, "hid", None),
        P("groups", None, None),
        P("groups", None, None),
        P("groups", None),
    )
    out_specs = P("groups", "hid", None)
    return jax.shard_map(body, mesh=mesh, in_specs=in_specs, out_specs=out_specs, check_vma=False)
```

```python
import functools

import jax
import jax.numpy as jnp
from jax import lax
from jax.experimental import pallas as pl
from jax.experimental.pallas import tpu as pltpu
from jax.sharding import PartitionSpec as P

MIB = 1 << 20
SCOPED = 10
VMEM = pl.BlockSpec(memory_space=pltpu.VMEM)
ANY = pl.BlockSpec(memory_space=pl.ANY)
BF16, F32 = jnp.bfloat16, jnp.float32


def in_vmem(x):
    return pltpu.with_memory_space_constraint(x, pltpu.VMEM)


def in_hbm(x):
    return pltpu.with_memory_space_constraint(x, pltpu.HBM)


def cost(flops, size):
    return pl.CostEstimate(flops=flops, bytes_accessed=size, transcendentals=0)


def swap(x, mask):
    n = lax.axis_size("hid")
    return lax.ppermute(x, "hid", [(i, i ^ mask) for i in range(n)])


def split_kernel(tokens_ref, *out_refs):
    steps, own, _ = tokens_ref.shape
    first = 0
    for out_ref in out_refs:
        columns = out_ref.shape[1]
        for s in range(steps):
            out_ref[s * own : (s + 1) * own] = tokens_ref[s, :, first : first + columns]
        first += columns


def split(tokens, widths):
    steps, own, _ = tokens.shape
    return pl.pallas_call(
        split_kernel,
        in_specs=[VMEM],
        out_specs=[VMEM] * len(widths),
        out_shape=[pltpu.VMEM((steps * own, w), tokens.dtype) for w in widths],
        compiler_params=pltpu.CompilerParams(vmem_limit_bytes=2 * MIB),
        cost_estimate=cost(0, 4 * tokens.size),
        name="split",
    )(in_vmem(tokens))


def stack_kernel(places, *refs):
    *part_refs, out_ref = refs[: len(places)] + refs[-1:]
    for part_ref, (column, rows) in zip(part_refs, places):
        columns = part_ref.shape[1]
        per = part_ref.shape[0] // len(rows)
        for i, row in enumerate(rows):
            out_ref[row * per : (row + 1) * per, column : column + columns] = part_ref[i * per : (i + 1) * per]


def stack(parts, places, shape, after):
    return pl.pallas_call(
        functools.partial(stack_kernel, places),
        in_specs=[VMEM] * len(parts) + [ANY],
        out_specs=VMEM,
        out_shape=pltpu.VMEM(shape, parts[0].dtype),
        compiler_params=pltpu.CompilerParams(vmem_limit_bytes=2 * MIB),
        cost_estimate=cost(0, 4 * shape[0] * shape[1]),
        name="stack",
    )(*[in_vmem(part) for part in parts], after)


def load_kernel(e, w_ref, after_ref, out_ref, token_ref, sem):
    copy = pltpu.make_async_copy(w_ref.at[e], out_ref, sem)
    copy.start()
    token_ref[...] = jnp.zeros_like(token_ref)
    copy.wait()


def load(w, e, after):
    return pl.pallas_call(
        functools.partial(load_kernel, e),
        in_specs=[ANY, ANY],
        out_specs=[VMEM, VMEM],
        out_shape=[pltpu.VMEM(w.shape[1:], w.dtype), pltpu.VMEM((8, 128), F32)],
        scratch_shapes=[pltpu.SemaphoreType.DMA],
        compiler_params=pltpu.CompilerParams(vmem_limit_bytes=2 * MIB),
        cost_estimate=cost(0, 2 * w.size // w.shape[0]),
        name="load",
    )(in_hbm(w), after)


def place_of(row, n, steps, own, me):
    per = steps * own
    slot, rest = row // per, row % per
    far = n // 4
    mask = slot // (2 * far) + 2 * ((slot // far) % 2) + 4 * (slot % far)
    return (rest // own) * (n * own) + (me ^ mask) * own + rest % own


def plan_kernel(n, own, ids_ref, weights_ref, return_ref, after_ref, route_ref, order_ref):
    steps, total = return_ref.shape
    rows = steps * total
    me = lax.axis_index("hid")
    down = lax.broadcasted_iota(jnp.int32, (rows, total), 0)
    place = place_of(down, n, steps, own, me)
    across = lax.broadcasted_iota(jnp.int32, (rows, total), 1)
    picked = [jnp.zeros((rows, total), F32)] * 5
    for s in range(steps):
        here = place == across + s * total
        values = [ids_ref[s, 0:1], ids_ref[s, 1:2], weights_ref[s, 0:1], weights_ref[s, 1:2], return_ref[s : s + 1]]
        picked = [jnp.where(here, value.astype(F32), old) for value, old in zip(values, picked)]
    first, second, first_weight, second_weight, source = [jnp.sum(p, axis=1, keepdims=True) for p in picked]
    for e in range(route_ref.shape[0]):
        route_ref[e] = jnp.where(first == e, first_weight, 0.0) + jnp.where(second == e, second_weight, 0.0)
    shape = (rows, rows)
    step = (lax.broadcasted_iota(jnp.int32, (rows, 1), 0) % (steps * own)) // own
    across = lax.broadcasted_iota(jnp.int32, shape, 1)
    order_ref[...] = (place_of(across, n, steps, own, me) == source.astype(jnp.int32) + step * total).astype(BF16)


def plan(expert_ids, gate_weights, return_order, experts, n, own, after):
    steps, total = return_order.shape
    rows = steps * total
    return pl.pallas_call(
        functools.partial(plan_kernel, n, own),
        in_specs=[VMEM] * 3 + [ANY],
        out_specs=[VMEM, VMEM],
        out_shape=[pltpu.VMEM((experts, rows, 1), F32), pltpu.VMEM((rows, rows), BF16)],
        compiler_params=pltpu.CompilerParams(vmem_limit_bytes=8 * MIB),
        cost_estimate=cost(0, 4 * rows * rows),
        name="plan",
    )(jnp.swapaxes(expert_ids, 1, 2), jnp.swapaxes(gate_weights, 1, 2), return_order, after)


def experts_kernel(
    half_ref, other_ref, route_ref, order_ref, gate_ref, up_ref, down_ref, *refs
):
    early = len(refs) // 2 - 3
    keep_ref, send_ref = refs[early : early + 2]
    homes = list(refs[early + 2 : 2 * early + 2])
    x_ref, h_ref, up_buf, up_sem, down_sem = refs[2 * early + 2 :]
    half, width = half_ref.shape
    experts, units, _ = down_ref.shape
    depth = experts * units
    blocks = width // units
    fit = width // depth
    homes.append(up_buf)
    homes += homes[: experts - early - 1]
    up_copies = {e: pltpu.make_async_copy(up_ref.at[e], homes[e], up_sem.at[e]) for e in range(early, experts)}
    down_homes = homes[experts - early - 1 : experts]
    down_homes = [ref.at[pl.ds(i * experts, experts)] for ref in down_homes for i in range(fit)]
    slots = len(down_homes)

    def block_copy(b):
        return pltpu.make_async_copy(
            down_ref.at[:, :, pl.ds(b * units, units)], down_homes[b % slots], down_sem.at[b % slots]
        )

    def start_blocks(first, last):
        for b in range(first, min(last, blocks)):
            block_copy(b).start()

    up_copies[early].start()
    x_ref[:half] = half_ref[...]
    x_ref[half:] = other_ref[...]
    for e in range(experts):
        gate = jnp.dot(x_ref[...], gate_ref[e], preferred_element_type=F32)
        if e in up_copies:
            up_copies[e].wait()
        up = jnp.dot(x_ref[...], homes[e].reshape(width, units)[...], preferred_element_type=F32)
        if e + early + 1 < experts:
            up_copies[e + early + 1].start()
        else:
            first = (e + early + 1 - experts) * fit
            start_blocks(first, min(first + fit, slots))
        hidden = gate / (1.0 + jnp.exp(-gate)) * up * route_ref[e]
        hidden = jnp.dot(order_ref[...], hidden.astype(BF16), preferred_element_type=F32)
        h_ref[:, e * units : (e + 1) * units] = hidden.astype(BF16)
    for b in range(blocks):
        block_copy(b).wait()
        w = down_homes[b % slots].reshape(depth, units)
        total = jnp.dot(h_ref[...], w[...], preferred_element_type=F32)
        start_blocks(b + slots, b + slots + 1)
        keep_ref[:, b * units : (b + 1) * units] = total[:half]
        send_ref[:, b * units : (b + 1) * units] = total[half:].astype(BF16)


def experts_of(half, other, route, order, w_gate, w_up, w_down, early):
    experts, units, width = w_down.shape
    rows = 2 * half.shape[0]
    keep, send, *_ = pl.pallas_call(
        experts_kernel,
        in_specs=[VMEM] * 5 + [ANY] * 2 + [VMEM] * len(early),
        out_specs=[VMEM] * (2 + len(early)),
        out_shape=[pltpu.VMEM((rows // 2, width), F32), pltpu.VMEM((rows // 2, width), BF16)]
        + [pltpu.VMEM(w.shape, w.dtype) for w in early],
        scratch_shapes=[
            pltpu.VMEM((rows, width), BF16),
            pltpu.VMEM((rows, experts * units), BF16),
            pltpu.VMEM(early[0].shape, BF16),
            pltpu.SemaphoreType.DMA((experts,)),
            pltpu.SemaphoreType.DMA((width // units,)),
        ],
        input_output_aliases={7 + i: 2 + i for i in range(len(early))},
        compiler_params=pltpu.CompilerParams(vmem_limit_bytes=SCOPED * MIB),
        cost_estimate=cost(0, 8 * w_down.size),
        name="experts",
    )(
        in_vmem(half), in_vmem(other), in_vmem(route), in_vmem(order), in_vmem(w_gate), in_hbm(w_up), in_hbm(w_down),
        *[in_vmem(w) for w in early],
    )
    return keep, send


def add_kernel(first, groups, keep_ref, *refs):
    got_refs, out_refs = refs[: -len(groups)], refs[-len(groups) :]
    per = out_refs[0].shape[0] // len(groups[0])
    columns = slice(first, first + out_refs[0].shape[1])
    for group, out_ref in zip(groups, out_refs):
        for i, block in enumerate(group):
            rows = slice(block * per, (block + 1) * per)
            total = keep_ref[rows, columns]
            for got_ref in got_refs:
                total = total + got_ref[rows, columns].astype(F32)
            out_ref[i * per : (i + 1) * per] = total.astype(out_ref.dtype)


def add(keep, gots, first, columns, groups):
    per = keep.shape[0] // sum(len(group) for group in groups)
    return pl.pallas_call(
        functools.partial(add_kernel, first, groups),
        in_specs=[VMEM] * (1 + len(gots)),
        out_specs=[VMEM] * len(groups),
        out_shape=[pltpu.VMEM((per * len(g), columns), BF16 if i else F32) for i, g in enumerate(groups)],
        compiler_params=pltpu.CompilerParams(vmem_limit_bytes=2 * MIB),
        cost_estimate=cost(0, 8 * keep.shape[0] * columns),
        name="add",
    )(in_vmem(keep), *[in_vmem(got) for got in gots])


def sum_kernel(far, *refs):
    *part_refs, out_ref = refs
    first = 0
    steps, own, _ = out_ref.shape
    for keep_ref, got_refs in ((part_refs[0], part_refs[1:far]), (part_refs[far], part_refs[far + 1 :])):
        total = keep_ref[...]
        for got_ref in got_refs:
            total = total + got_ref[...].astype(F32)
        total = total.astype(out_ref.dtype)
        columns = keep_ref.shape[1]
        for s in range(steps):
            out_ref[s, :, first : first + columns] = total[s * own : (s + 1) * own]
        first += columns


def body(tokens, w_gate, w_up, w_down, expert_ids, gate_weights, return_order):
    steps, own, width = tokens.shape
    experts, _, units = w_gate.shape
    n = lax.axis_size("hid")
    far = n // 4
    per = steps * own
    rows = per * n
    a = width * 3 // 4
    b = width - a
    xa, xb = split(tokens, [a, b])
    za = [swap(xa, 4 * z) for z in range(1, far)]
    yb = swap(xb, 2)
    w_up = w_up.reshape(experts, width // units, units, units)
    up0, ready = load(w_up, 0, xa)
    xb = stack([xb, yb], [(0, [0]), (0, [1])], (2 * per, b), ready)
    zb = [swap(xb, 4 * z) for z in range(1, far)]
    xa = stack([xa] + za, [(0, [z]) for z in range(far)], (far * per, a), xb)
    ya = swap(xa, 2)
    up1, ready = load(w_up, 1, xa)
    route, order = plan(expert_ids, gate_weights, return_order, experts, n, own, ready)
    half = stack(
        [xa, ya, xb] + zb,
        [(0, [0]), (0, [1])] + [(a, [z, far + z]) for z in range(far)],
        (2 * far * per, width),
        order,
    )
    other = swap(half, 1)
    keep, send = experts_of(half, other, route, order, w_gate, w_up, w_down, [up0, up1])

    a = width * 7 // 12
    b = width - a
    got = swap(send, 1)
    keep_a, send_a = add(keep, [got], 0, a, [list(range(far)), list(range(far, 2 * far))])
    got_a = swap(send_a, 2)
    keep_b, *send_b = add(keep, [got], a, b, [[z, far + z] for z in range(far)])
    got_b = [swap(send, 4 * (z + 1)) for z, send in enumerate(send_b)]
    keep_a, *send_a = add(keep_a, [got_a], 0, a, [[z] for z in range(far)])
    got_a = [swap(send, 4 * (z + 1)) for z, send in enumerate(send_a)]
    keep_b, send_b = add(keep_b, got_b, 0, b, [[0], [1]])
    parts = [keep_a, *got_a, keep_b, swap(send_b, 2)]
    return pl.pallas_call(
        functools.partial(sum_kernel, far),
        in_specs=[VMEM] * len(parts),
        out_specs=VMEM,
        out_shape=jax.ShapeDtypeStruct(tokens.shape, tokens.dtype),
        compiler_params=pltpu.CompilerParams(vmem_limit_bytes=4 * MIB),
        cost_estimate=cost(0, 4 * tokens.size),
        name="sum",
    )(*[in_vmem(part) for part in parts])


def solution(mesh):
    in_specs = (
        P("groups", "hid", None),
        P(None, None, "hid"),
        P(None, None, "hid"),
        P(None, "hid", None),
        P("groups", None, None),
        P("groups", None, None),
        P("groups", None),
    )
    out_specs = P("groups", "hid", None)
    return jax.shard_map(body, mesh=mesh, in_specs=in_specs, out_specs=out_specs, check_vma=False)
```

```python
import functools

import jax
import jax.numpy as jnp
from jax import lax
from jax.experimental import pallas as pl
from jax.experimental.pallas import tpu as pltpu
from jax.sharding import PartitionSpec as P

MIB = 1 << 20
SCOPED = 10
VMEM = pl.BlockSpec(memory_space=pltpu.VMEM)
ANY = pl.BlockSpec(memory_space=pl.ANY)
BF16, F32 = jnp.bfloat16, jnp.float32


def in_vmem(x):
    return pltpu.with_memory_space_constraint(x, pltpu.VMEM)


def in_hbm(x):
    return pltpu.with_memory_space_constraint(x, pltpu.HBM)


def cost(flops, size):
    return pl.CostEstimate(flops=flops, bytes_accessed=size, transcendentals=0)


def swap(x, mask):
    n = lax.axis_size("hid")
    return lax.ppermute(x, "hid", [(i, i ^ mask) for i in range(n)])


def split_kernel(tokens_ref, *out_refs):
    steps, own, _ = tokens_ref.shape
    first = 0
    for out_ref in out_refs:
        columns = out_ref.shape[1]
        for s in range(steps):
            out_ref[s * own : (s + 1) * own] = tokens_ref[s, :, first : first + columns]
        first += columns


def split(tokens, widths):
    steps, own, _ = tokens.shape
    return pl.pallas_call(
        split_kernel,
        in_specs=[VMEM],
        out_specs=[VMEM] * len(widths),
        out_shape=[pltpu.VMEM((steps * own, w), tokens.dtype) for w in widths],
        compiler_params=pltpu.CompilerParams(vmem_limit_bytes=2 * MIB),
        cost_estimate=cost(0, 4 * tokens.size),
        name="split",
    )(in_vmem(tokens))


def stack_kernel(places, *refs):
    *part_refs, out_ref = refs[: len(places)] + refs[-1:]
    for part_ref, (column, rows) in zip(part_refs, places):
        columns = part_ref.shape[1]
        per = part_ref.shape[0] // len(rows)
        for i, row in enumerate(rows):
            out_ref[row * per : (row + 1) * per, column : column + columns] = part_ref[i * per : (i + 1) * per]


def stack(parts, places, shape, after):
    return pl.pallas_call(
        functools.partial(stack_kernel, places),
        in_specs=[VMEM] * len(parts) + [ANY],
        out_specs=VMEM,
        out_shape=pltpu.VMEM(shape, parts[0].dtype),
        compiler_params=pltpu.CompilerParams(vmem_limit_bytes=2 * MIB),
        cost_estimate=cost(0, 4 * shape[0] * shape[1]),
        name="stack",
    )(*[in_vmem(part) for part in parts], after)


def load_kernel(e, w_ref, after_ref, out_ref, token_ref, sem):
    copy = pltpu.make_async_copy(w_ref.at[e], out_ref, sem)
    copy.start()
    token_ref[...] = jnp.zeros_like(token_ref)
    copy.wait()


def load(w, e, after):
    return pl.pallas_call(
        functools.partial(load_kernel, e),
        in_specs=[ANY, ANY],
        out_specs=[VMEM, VMEM],
        out_shape=[pltpu.VMEM(w.shape[1:], w.dtype), pltpu.VMEM((8, 128), F32)],
        scratch_shapes=[pltpu.SemaphoreType.DMA],
        compiler_params=pltpu.CompilerParams(vmem_limit_bytes=2 * MIB),
        cost_estimate=cost(0, 2 * w.size // w.shape[0]),
        name="load",
    )(in_hbm(w), after)


def place_of(row, n, steps, own, me):
    per = steps * own
    slot, rest = row // per, row % per
    far = n // 4
    mask = slot // (2 * far) + 2 * ((slot // far) % 2) + 4 * (slot % far)
    return (rest // own) * (n * own) + (me ^ mask) * own + rest % own


def plan_kernel(n, own, ids_ref, weights_ref, return_ref, after_ref, route_ref, order_ref):
    steps, total = return_ref.shape
    rows = steps * total
    me = lax.axis_index("hid")
    down = lax.broadcasted_iota(jnp.int32, (rows, total), 0)
    place = place_of(down, n, steps, own, me)
    across = lax.broadcasted_iota(jnp.int32, (rows, total), 1)
    picked = [jnp.zeros((rows, total), F32)] * 5
    for s in range(steps):
        here = place == across + s * total
        values = [ids_ref[s, 0:1], ids_ref[s, 1:2], weights_ref[s, 0:1], weights_ref[s, 1:2], return_ref[s : s + 1]]
        picked = [jnp.where(here, value.astype(F32), old) for value, old in zip(values, picked)]
    first, second, first_weight, second_weight, source = [jnp.sum(p, axis=1, keepdims=True) for p in picked]
    for e in range(route_ref.shape[0]):
        route_ref[e] = jnp.where(first == e, first_weight, 0.0) + jnp.where(second == e, second_weight, 0.0)
    shape = (rows, rows)
    step = (lax.broadcasted_iota(jnp.int32, (rows, 1), 0) % (steps * own)) // own
    across = lax.broadcasted_iota(jnp.int32, shape, 1)
    order_ref[...] = (place_of(across, n, steps, own, me) == source.astype(jnp.int32) + step * total).astype(BF16)


def plan(expert_ids, gate_weights, return_order, experts, n, own, after):
    steps, total = return_order.shape
    rows = steps * total
    return pl.pallas_call(
        functools.partial(plan_kernel, n, own),
        in_specs=[VMEM] * 3 + [ANY],
        out_specs=[VMEM, VMEM],
        out_shape=[pltpu.VMEM((experts, rows, 1), F32), pltpu.VMEM((rows, rows), BF16)],
        compiler_params=pltpu.CompilerParams(vmem_limit_bytes=8 * MIB),
        cost_estimate=cost(0, 4 * rows * rows),
        name="plan",
    )(jnp.swapaxes(expert_ids, 1, 2), jnp.swapaxes(gate_weights, 1, 2), return_order, after)


def experts_kernel(
    half_ref, other_ref, route_ref, order_ref, gate_ref, up_ref, down_ref, *refs
):
    early = len(refs) // 2 - 4
    keep_ref, *send_refs = refs[early : early + 3]
    homes = list(refs[early + 3 : 2 * early + 3])
    x_ref, h_ref, up_buf, up_sem, down_sem = refs[2 * early + 3 :]
    half, width = half_ref.shape
    experts, units, _ = down_ref.shape
    depth = experts * units
    blocks = width // units
    fit = width // depth
    homes.append(up_buf)
    homes += homes[: experts - early - 1]
    up_copies = {e: pltpu.make_async_copy(up_ref.at[e], homes[e], up_sem.at[e]) for e in range(early, experts)}
    down_homes = homes[experts - early - 1 : experts]
    down_homes = [ref.at[pl.ds(i * experts, experts)] for ref in down_homes for i in range(fit)]
    slots = len(down_homes)

    def block_copy(b):
        return pltpu.make_async_copy(
            down_ref.at[:, :, pl.ds(b * units, units)], down_homes[b % slots], down_sem.at[b % slots]
        )

    def start_blocks(first, last):
        for b in range(first, min(last, blocks)):
            block_copy(b).start()

    up_copies[early].start()
    x_ref[:half] = half_ref[...]
    x_ref[half:] = other_ref[...]
    for e in range(experts):
        gate = jnp.dot(x_ref[...], gate_ref[e], preferred_element_type=F32)
        if e in up_copies:
            up_copies[e].wait()
        up = jnp.dot(x_ref[...], homes[e].reshape(width, units)[...], preferred_element_type=F32)
        if e + early + 1 < experts:
            up_copies[e + early + 1].start()
        else:
            first = (e + early + 1 - experts) * fit
            start_blocks(first, min(first + fit, slots))
        hidden = gate / (1.0 + jnp.exp(-gate)) * up * route_ref[e]
        hidden = jnp.dot(order_ref[...], hidden.astype(BF16), preferred_element_type=F32)
        h_ref[:, e * units : (e + 1) * units] = hidden.astype(BF16)
    for b in range(blocks):
        block_copy(b).wait()
        w = down_homes[b % slots].reshape(depth, units)
        total = jnp.dot(h_ref[...], w[...], preferred_element_type=F32)
        start_blocks(b + slots, b + slots + 1)
        keep_ref[:, b * units : (b + 1) * units] = total[:half]
        send_ref, at = send_refs[0], b * units
        if at >= send_ref.shape[1]:
            send_ref, at = send_refs[1], at - send_ref.shape[1]
        send_ref[:, at : at + units] = total[half:].astype(BF16)


def experts_of(half, other, route, order, w_gate, w_up, w_down, early, cut):
    experts, units, width = w_down.shape
    rows = 2 * half.shape[0]
    keep, first, second, *_ = pl.pallas_call(
        experts_kernel,
        in_specs=[VMEM] * 5 + [ANY] * 2 + [VMEM] * len(early),
        out_specs=[VMEM] * (3 + len(early)),
        out_shape=[pltpu.VMEM((rows // 2, width), F32)]
        + [pltpu.VMEM((rows // 2, columns), BF16) for columns in (cut, width - cut)]
        + [pltpu.VMEM(w.shape, w.dtype) for w in early],
        scratch_shapes=[
            pltpu.VMEM((rows, width), BF16),
            pltpu.VMEM((rows, experts * units), BF16),
            pltpu.VMEM(early[0].shape, BF16),
            pltpu.SemaphoreType.DMA((experts,)),
            pltpu.SemaphoreType.DMA((width // units,)),
        ],
        input_output_aliases={7 + i: 3 + i for i in range(len(early))},
        compiler_params=pltpu.CompilerParams(vmem_limit_bytes=SCOPED * MIB),
        cost_estimate=cost(0, 8 * w_down.size),
        name="experts",
    )(
        in_vmem(half), in_vmem(other), in_vmem(route), in_vmem(order), in_vmem(w_gate), in_hbm(w_up), in_hbm(w_down),
        *[in_vmem(w) for w in early],
    )
    return keep, first, second


def add_kernel(first, groups, keep_ref, *refs):
    got_refs, out_refs = refs[: -len(groups)], refs[-len(groups) :]
    per = out_refs[0].shape[0] // len(groups[0])
    columns = slice(first, first + out_refs[0].shape[1])
    for group, out_ref in zip(groups, out_refs):
        for i, block in enumerate(group):
            rows = slice(block * per, (block + 1) * per)
            total = keep_ref[rows, columns]
            for got_ref in got_refs:
                same = columns if got_ref.shape == keep_ref.shape else slice(None)
                total = total + got_ref[rows, same].astype(F32)
            out_ref[i * per : (i + 1) * per] = total.astype(out_ref.dtype)


def add(keep, gots, first, columns, groups):
    per = keep.shape[0] // sum(len(group) for group in groups)
    return pl.pallas_call(
        functools.partial(add_kernel, first, groups),
        in_specs=[VMEM] * (1 + len(gots)),
        out_specs=[VMEM] * len(groups),
        out_shape=[pltpu.VMEM((per * len(g), columns), BF16 if i else F32) for i, g in enumerate(groups)],
        compiler_params=pltpu.CompilerParams(vmem_limit_bytes=2 * MIB),
        cost_estimate=cost(0, 8 * keep.shape[0] * columns),
        name="add",
    )(in_vmem(keep), *[in_vmem(got) for got in gots])


def sum_kernel(far, *refs):
    *part_refs, out_ref = refs
    first = 0
    steps, own, _ = out_ref.shape
    for keep_ref, got_refs in ((part_refs[0], part_refs[1:far]), (part_refs[far], part_refs[far + 1 :])):
        total = keep_ref[...]
        for got_ref in got_refs:
            total = total + got_ref[...].astype(F32)
        total = total.astype(out_ref.dtype)
        columns = keep_ref.shape[1]
        for s in range(steps):
            out_ref[s, :, first : first + columns] = total[s * own : (s + 1) * own]
        first += columns


def body(tokens, w_gate, w_up, w_down, expert_ids, gate_weights, return_order):
    steps, own, width = tokens.shape
    experts, _, units = w_gate.shape
    n = lax.axis_size("hid")
    far = n // 4
    per = steps * own
    rows = per * n
    a = width * 3 // 4
    b = width - a
    xa, xb = split(tokens, [a, b])
    za = [swap(xa, 4 * z) for z in range(1, far)]
    yb = swap(xb, 2)
    w_up = w_up.reshape(experts, width // units, units, units)
    up0, ready = load(w_up, 0, xa)
    xb = stack([xb, yb], [(0, [0]), (0, [1])], (2 * per, b), ready)
    zb = [swap(xb, 4 * z) for z in range(1, far)]
    xa = stack([xa] + za, [(0, [z]) for z in range(far)], (far * per, a), xb)
    ya = swap(xa, 2)
    up1, ready = load(w_up, 1, xa)
    route, order = plan(expert_ids, gate_weights, return_order, experts, n, own, ready)
    half = stack(
        [xa, ya, xb] + zb,
        [(0, [0]), (0, [1])] + [(a, [z, far + z]) for z in range(far)],
        (2 * far * per, width),
        order,
    )
    other = swap(half, 1)
    cut = units * (width // units * 7 // 12)
    keep, send_a, send_b = experts_of(half, other, route, order, w_gate, w_up, w_down, [up0, up1], cut)

    a, b = cut, width - cut
    got_a, got_b = swap(send_a, 1), swap(send_b, 1)
    keep_a, send_a = add(keep, [got_a], 0, a, [list(range(far)), list(range(far, 2 * far))])
    got_a = swap(send_a, 2)
    keep_b, *send_b = add(keep, [got_b], a, b, [[z, far + z] for z in range(far)])
    got_b = [swap(send, 4 * (z + 1)) for z, send in enumerate(send_b)]
    keep_a, *send_a = add(keep_a, [got_a], 0, a, [[z] for z in range(far)])
    got_a = [swap(send, 4 * (z + 1)) for z, send in enumerate(send_a)]
    keep_b, send_b = add(keep_b, got_b, 0, b, [[0], [1]])
    parts = [keep_a, *got_a, keep_b, swap(send_b, 2)]
    return pl.pallas_call(
        functools.partial(sum_kernel, far),
        in_specs=[VMEM] * len(parts),
        out_specs=VMEM,
        out_shape=jax.ShapeDtypeStruct(tokens.shape, tokens.dtype),
        compiler_params=pltpu.CompilerParams(vmem_limit_bytes=4 * MIB),
        cost_estimate=cost(0, 4 * tokens.size),
        name="sum",
    )(*[in_vmem(part) for part in parts])


def solution(mesh):
    in_specs = (
        P("groups", "hid", None),
        P(None, None, "hid"),
        P(None, None, "hid"),
        P(None, "hid", None),
        P("groups", None, None),
        P("groups", None, None),
        P("groups", None),
    )
    out_specs = P("groups", "hid", None)
    return jax.shard_map(body, mesh=mesh, in_specs=in_specs, out_specs=out_specs, check_vma=False)
```
